32 devices in a mesh: groups: 2 (over y), seq: 4 (over z), dp: 4 (over x, core).
Axes of the slice: x: 2, y: 2, z: 4, core: 2. Of those that a mesh axis runs over, the one named last changes fastest.
Arguments:
- inputs: bfloat16 [8, 65536, 512], P(('groups', 'dp'), 'seq'), parts along dimension 0, may hold values from -6 to 6
- cotangent: bfloat16 [8, 65536, 512], P(('groups', 'dp'), 'seq'), parts along dimension 0, may hold values from -6 to 6
- first_factor: bfloat16 [256, 256, 256], P('seq', 'dp'), may hold values from -0.375 to 0.375
- second_factor: bfloat16 [256, 256, 256], P('seq', 'dp'), may hold values from -0.375 to 0.375
Outputs:
- mixed_out: bfloat16 [8, 65536, 512], P(('groups', 'dp'), 'seq'), parts along dimension 0
- input_grad: bfloat16 [8, 65536, 512], P(('groups', 'dp'), 'seq'), parts along dimension 0
- first_factor_grad: bfloat16 [512, 256, 256], P(('groups', 'seq'), 'dp'), parts along dimension 0
- second_factor_grad: bfloat16 [512, 256, 256], P(('groups', 'seq'), 'dp'), parts along dimension 0
The draws below stay inside these ranges and needn't reach their ends.
There are 2 independent parts, one for each index of `groups`. The reference program is written for one: setup_inputs(seed, part) draws one part's arguments, and reference() takes and returns one part's arrays. A program takes and returns all parts, laid end to end along the dimension named above; an argument that names none is the same for every part. Nothing has to cross between parts.
All inputs are finite; a program needn't handle non-finite values.
Results may differ from the reference program's by a relative error of at most 0.009.
Values may be sent and summed in bfloat16 or wider, within the bound.
A program may use at most 320 MiB of HBM per device.

```python
import math
import jax
import jax.numpy as jnp
from jax import lax

C = 512
BLK = 256
NBK = 256
SEQ_DEV = 1
LENGTH = 65536
BATCH = 4
N_DP = 4


def block_levels(key, extent, pieces, least, largest):
    factor_of = 1.0
    for dim, parts in pieces:
        steps = jax.random.uniform(jax.random.fold_in(jax.random.fold_in(key, 6), dim), (parts,), jnp.float32, least / len(pieces), largest / len(pieces))
        factor_of = factor_of * jnp.repeat(jnp.exp(steps), extent[dim] // parts).reshape((-1,) + (1,) * (len(extent) - 1 - dim))
    return factor_of


def gaussian(stream_key, shape, width, reach, split=(), kind=jnp.bfloat16):
    factor_of = block_levels(stream_key, shape, split, -0.22, 0.18) if split else 1.0
    result = jax.random.normal(stream_key, shape, jnp.float32) * width * factor_of
    return jnp.minimum(jnp.maximum(result, -reach), reach).astype(kind)


def setup_inputs(seed: int = 0, part: int = 0) -> dict:
    keys = jax.random.split(jax.random.key(seed), 5)
    part_splits = jax.random.split(jax.random.fold_in(keys[4], part), 5)
    return {
        "inputs": gaussian(part_splits[0], (BATCH, LENGTH, C), 1.0, 6.0, ((0, 4), (1, 4))),
        "cotangent": gaussian(part_splits[1], (BATCH, LENGTH, C), 1.0, 6.0, ((0, 4), (1, 4))),
        "first_factor": gaussian(keys[2], (NBK, BLK, BLK), BLK ** -0.5, 0.375, ((0, 4), (1, 4))),
        "second_factor": gaussian(keys[3], (BLK, NBK, NBK), NBK ** -0.5, 0.375, ((0, 4), (1, 4))),
    }


def silu_parts(values):
    sig = jax.nn.sigmoid(values)
    return (values * sig, sig * (1.0 + values * (1.0 - sig)))

def reference(inputs, cotangent, first_factor, second_factor):
    first_f32 = first_factor.astype(jnp.float32)
    second_f32 = second_factor.astype(jnp.float32)
    norm_scale = 1.0 / math.sqrt(BATCH * C)

    def replica(pair):
        x_rows, cot_rows = pair
        blocked = x_rows.reshape(SEQ_DEV, NBK, BLK, C).astype(jnp.float32)
        first_out = jnp.einsum('ijk,bikc->bijc', first_f32, blocked).astype(jnp.bfloat16)
        first_use = first_out.astype(jnp.float32)
        mixing = jnp.einsum('jik,bkjc->bjic', second_f32, first_use).reshape(SEQ_DEV, LENGTH, C)
        gate_value, gate_slope = silu_parts(x_rows.astype(jnp.float32))
        mixed_out = (mixing * gate_value).astype(jnp.bfloat16)
        cot_f32 = cot_rows.astype(jnp.float32)
        gated_cot = (cot_f32 * gate_value).astype(jnp.bfloat16).reshape(SEQ_DEV, BLK, NBK, C).astype(jnp.float32)
        part_two = (norm_scale * jnp.einsum('bjic,bkjc->jik', gated_cot, first_use)).astype(jnp.bfloat16)
        back_sent = jnp.einsum('jik,bjic->bkjc', second_f32, gated_cot).astype(jnp.bfloat16).astype(jnp.float32)
        part_one = (norm_scale * jnp.einsum('bijc,bikc->ijk', back_sent, blocked)).astype(jnp.bfloat16)
        local_grad = jnp.einsum('ijk,bijc->bikc', first_f32, back_sent).reshape(SEQ_DEV, LENGTH, C)
        input_grad = (local_grad + cot_f32 * mixing * gate_slope).astype(jnp.bfloat16)
        return (mixed_out, input_grad, part_one, part_two)
    x_groups = inputs.reshape(N_DP, SEQ_DEV, LENGTH, C)
    cot_groups = cotangent.reshape(N_DP, SEQ_DEV, LENGTH, C)
    outs_all, grads_all, parts_one, parts_two = lax.map(replica, (x_groups, cot_groups))
    mixed_out = outs_all.reshape(BATCH, LENGTH, C)
    input_grad = grads_all.reshape(BATCH, LENGTH, C)
    first_grad = lax.optimization_barrier(jnp.sum(parts_one.astype(jnp.float32), axis=0)).astype(jnp.bfloat16)
    second_grad = lax.optimization_barrier(jnp.sum(parts_two.astype(jnp.float32), axis=0)).astype(jnp.bfloat16)
    return (mixed_out, input_grad, first_grad, second_grad)
```

```python
import math

import jax
import jax.numpy as jnp
from jax import lax
from jax.experimental.layout import Layout, with_layout_constraint
from jax.sharding import PartitionSpec as P


def silu_parts(values):
    sig = jax.nn.sigmoid(values)
    return (values * sig, sig * (1.0 + values * (1.0 - sig)))


def row_major(value):
    return with_layout_constraint(value, Layout(tuple(range(value.ndim))))


def scatter_rows(parts):
    blocks, ring, rows, columns = parts.shape
    flat = parts.reshape(blocks, ring * rows, columns)
    kept = lax.psum_scatter(flat, "dp", scatter_dimension=1, tiled=True)
    return kept.reshape(blocks, kept.shape[1] // rows, rows, columns)


def shards(inputs, cotangent, first_factor, second_factor):
    f32, bf16 = jnp.float32, jnp.bfloat16
    seqs = inputs.shape[0]
    rows = inputs.shape[1]
    channels = inputs.shape[2]
    ring = lax.axis_size("seq")
    blocks = first_factor.shape[0]
    columns = second_factor.shape[0]
    width = first_factor.shape[2]
    width_two = second_factor.shape[2]
    norm_scale = 1.0 / math.sqrt(lax.axis_size("dp") * seqs * channels)
    chunks = math.gcd(4, math.gcd(blocks, columns))
    ic, jc = blocks // chunks, columns // chunks

    blocked = inputs.reshape(seqs, blocks, width, channels)
    cot_f32 = cotangent.astype(f32)
    gate_value, gate_slope = silu_parts(inputs.astype(f32))

    def after(value, *others):
        kept = lax.optimization_barrier((value,) + others)
        return kept[0], kept[1:]

    def exchange(part):
        return lax.all_to_all(part, "seq", split_axis=0, concat_axis=0, tiled=True)

    first_parts, received = [], []
    for q in range(chunks):
        own = slice(q * ic, (q + 1) * ic)
        factor = lax.all_gather(first_factor[own], "dp", axis=1, tiled=True)
        first_parts.append(factor)
        part = jnp.einsum(
            "ijk,bikc->bijc", factor, blocked[:, own], preferred_element_type=f32
        ).astype(bf16)
        part = part.reshape(seqs, ic, ring, columns, channels).transpose(2, 0, 1, 3, 4)
        part = row_major(part)
        if q:
            part, (received[-1],) = after(part, received[-1])
        received.append(exchange(part))

    second_full = lax.all_gather(second_factor, "dp", axis=1, tiled=True)
    gated_cot = (
        (cot_f32 * gate_value).astype(bf16).reshape(seqs, columns, width_two, channels)
    )
    previous = received
    returned = []
    first_full = jnp.concatenate(first_parts, axis=0)
    first_split = first_full.reshape(blocks, ring, chunks, jc, width)

    def through_first(q, total):
        back = returned[q]
        grad_one = norm_scale * jnp.einsum(
            "sbitc,bikc->istk", back, blocked, preferred_element_type=f32
        )
        total = total + jnp.einsum(
            "istk,sbitc->bikc", first_split[:, :, q], back, preferred_element_type=f32
        )
        return grad_one.astype(bf16), total

    grads_one = []
    done = 0
    for q in range(chunks):
        own = slice(q * jc, (q + 1) * jc)
        part = jnp.einsum(
            "jik,bjic->bkjc", second_full[own], gated_cot[:, own], preferred_element_type=f32
        ).astype(bf16)
        part = part.reshape(seqs, ring, blocks, jc, channels).transpose(1, 0, 2, 3, 4)
        part = row_major(part)
        if q == chunks // 2:
            exchanged = jnp.concatenate(received, axis=2).transpose(1, 0, 2, 3, 4)
            exchanged = exchanged.reshape(seqs, ring * blocks, columns, channels)
            mixing = jnp.einsum(
                "jik,bkjc->bjic", second_full, exchanged, preferred_element_type=f32
            ).reshape(seqs, rows, channels)
            outputs = (mixing * gate_value).astype(bf16)
            grad_two = norm_scale * jnp.einsum(
                "bjic,bkjc->jik", gated_cot, exchanged, preferred_element_type=f32
            )
            grad_two = grad_two.astype(bf16)
            total = (cot_f32 * mixing * gate_slope).reshape(blocked.shape)
            part, (outputs, grad_two, total) = after(part, outputs, grad_two, total)
            second_sum = lax.psum_scatter(
                grad_two, "dp", scatter_dimension=1, tiled=True
            )
        elif q > chunks // 2:
            while done < q - 1:
                grad_one, total = through_first(done, total)
                grads_one.append(grad_one)
                done += 1
            part, (total, *grads_one) = after(part, total, *grads_one)
            grads_one = list(grads_one)
        part, (previous[-1],) = after(part, previous[-1])
        returned.append(exchange(part))
        previous = returned

    while done < chunks - 1:
        grad_one, total = through_first(done, total)
        grads_one.append(grad_one)
        done += 1
    first_sums = []
    if grads_one:
        early = jnp.concatenate(grads_one, axis=2)
        early_sum = scatter_rows(early)
        returned[-1], (early_sum, total, second_sum) = after(
            returned[-1], early_sum, total, second_sum
        )
        first_sums.append(early_sum)
    grad_one, total = through_first(chunks - 1, total)
    first_sums.append(scatter_rows(grad_one))
    first_sum = jnp.concatenate(first_sums, axis=2).reshape(first_factor.shape)
    input_grad = total.reshape(seqs, rows, channels).astype(bf16)
    return (outputs, input_grad, first_sum, second_sum)


def solution(mesh):
    in_specs = (
        P(("groups", "dp"), "seq", None),
        P(("groups", "dp"), "seq", None),
        P("seq", "dp", None),
        P("seq", "dp", None),
    )
    out_specs = (
        P(("groups", "dp"), "seq", None),
        P(("groups", "dp"), "seq", None),
        P(("groups", "seq"), "dp", None),
        P(("groups", "seq"), "dp", None),
    )
    return jax.shard_map(shards, mesh=mesh, in_specs=in_specs, out_specs=out_specs, check_vma=False)
```

```python
import math

import jax
import jax.numpy as jnp
from jax import lax
from jax.experimental import pallas as pl
from jax.experimental.layout import Layout, with_layout_constraint
from jax.experimental.pallas import tpu as pltpu
from jax.sharding import PartitionSpec as P


def silu_parts(values):
    sig = jax.nn.sigmoid(values)
    return (values * sig, sig * (1.0 + values * (1.0 - sig)))


def add_back(total, factors, backs, out_type):
    blocks, width, channels = total.shape
    step = math.gcd(blocks, 4)
    count = len(backs)

    def kernel(*refs):
        total_ref, out_ref = refs[0], refs[-1]
        factor_refs, back_refs = refs[1 : 1 + count], refs[1 + count : 1 + 2 * count]
        for block in range(step):
            value = total_ref[block]
            for factor_ref, back_ref in zip(factor_refs, back_refs):
                sources = back_ref.shape[0]
                left = jnp.concatenate([factor_ref[block, n] for n in range(sources)], axis=0)
                right = jnp.concatenate([back_ref[n, block] for n in range(sources)], axis=0)
                value = value + lax.dot_general(
                    left, right, (((0,), (0,)), ((), ())), preferred_element_type=jnp.float32
                )
            out_ref[block] = value.astype(out_ref.dtype)

    whole = pl.BlockSpec((step, width, channels), lambda n: (n, 0, 0))
    sources, _, rows, _ = backs[0].shape
    return pl.pallas_call(
        kernel,
        grid=(blocks // step,),
        in_specs=[whole]
        + [pl.BlockSpec((step, sources, rows, width), lambda n: (n, 0, 0, 0))] * count
        + [pl.BlockSpec((sources, step, rows, channels), lambda n: (0, n, 0, 0))] * count,
        out_specs=whole,
        out_shape=jax.ShapeDtypeStruct(total.shape, out_type),
        compiler_params=pltpu.CompilerParams(vmem_limit_bytes=40 * 1024 * 1024),
        cost_estimate=pl.CostEstimate(
            flops=2 * count * blocks * sources * rows * width * channels,
            bytes_accessed=blocks * width * channels * 8,
            transcendentals=0,
        ),
    )(total, *factors, *backs)


def row_major(value):
    return with_layout_constraint(value, Layout(tuple(range(value.ndim))))


def scatter_rows(parts):
    blocks, ring, rows, columns = parts.shape
    flat = parts.reshape(blocks, ring * rows, columns)
    kept = lax.psum_scatter(flat, "dp", scatter_dimension=1, tiled=True)
    return kept.reshape(blocks, kept.shape[1] // rows, rows, columns)


def shards(inputs, cotangent, first_factor, second_factor):
    f32, bf16 = jnp.float32, jnp.bfloat16
    seqs = inputs.shape[0]
    rows = inputs.shape[1]
    channels = inputs.shape[2]
    ring = lax.axis_size("seq")
    blocks = first_factor.shape[0]
    columns = second_factor.shape[0]
    width = first_factor.shape[2]
    width_two = second_factor.shape[2]
    norm_scale = 1.0 / math.sqrt(lax.axis_size("dp") * seqs * channels)
    chunks = math.gcd(4, math.gcd(blocks, columns))
    ic, jc = blocks // chunks, columns // chunks

    blocked = inputs.reshape(seqs, blocks, width, channels)
    cot_f32 = cotangent.astype(f32)
    gate_value, gate_slope = silu_parts(inputs.astype(f32))

    def after(value, *others):
        kept = lax.optimization_barrier((value,) + others)
        return kept[0], kept[1:]

    def exchange(part):
        return lax.all_to_all(part, "seq", split_axis=0, concat_axis=0, tiled=True)

    first_parts, received = [], []
    for q in range(chunks):
        own = slice(q * ic, (q + 1) * ic)
        factor = lax.all_gather(first_factor[own], "dp", axis=1, tiled=True)
        first_parts.append(factor)
        part = jnp.einsum(
            "ijk,bikc->bijc", factor, blocked[:, own], preferred_element_type=f32
        ).astype(bf16)
        part = part.reshape(seqs, ic, ring, columns, channels).transpose(2, 0, 1, 3, 4)
        part = row_major(part)
        if q:
            part, (received[-1],) = after(part, received[-1])
        received.append(exchange(part))

    second_full = lax.all_gather(second_factor, "dp", axis=1, tiled=True)
    gated_cot = (
        (cot_f32 * gate_value).astype(bf16).reshape(seqs, columns, width_two, channels)
    )
    previous = received
    returned = []
    first_full = jnp.concatenate(first_parts, axis=0)
    first_split = first_full.reshape(blocks, ring, chunks, jc, width)

    def grad_of(q):
        grad_one = norm_scale * jnp.einsum(
            "sbitc,bikc->istk", returned[q], blocked, preferred_element_type=f32
        )
        return grad_one.astype(bf16)

    def through_first(some, total, out_type):
        factors = [first_split[:, :, q] for q in some]
        backs = [returned[q].reshape(ring, blocks, jc, channels) for q in some]
        if jc % 16:
            factors = [f.reshape(blocks, 1, ring * jc, width) for f in factors]
            backs = [
                g.transpose(1, 0, 2, 3).reshape(1, blocks, ring * jc, channels) for g in backs
            ]
        return add_back(total, factors, backs, out_type)

    for q in range(chunks):
        own = slice(q * jc, (q + 1) * jc)
        part = jnp.einsum(
            "jik,bjic->bkjc", second_full[own], gated_cot[:, own], preferred_element_type=f32
        ).astype(bf16)
        part = part.reshape(seqs, ring, blocks, jc, channels).transpose(1, 0, 2, 3, 4)
        part = row_major(part)
        if q == chunks // 2:
            exchanged = jnp.concatenate(received, axis=2).transpose(1, 0, 2, 3, 4)
            exchanged = exchanged.reshape(seqs, ring * blocks, columns, channels)
            mixing = jnp.einsum(
                "jik,bkjc->bjic", second_full, exchanged, preferred_element_type=f32
            ).reshape(seqs, rows, channels)
            mixing, (exchanged, returned[0]) = after(mixing, exchanged, returned[0])
            outputs = (mixing * gate_value).astype(bf16)
            grad_two = norm_scale * jnp.einsum(
                "bjic,bkjc->jik", gated_cot, exchanged, preferred_element_type=f32
            )
            grad_two = grad_two.astype(bf16)
            total = (cot_f32 * mixing * gate_slope).reshape(blocks, width, channels)
            part, (outputs, grad_two, total) = after(part, outputs, grad_two, total)
            second_sum = lax.psum_scatter(
                grad_two, "dp", scatter_dimension=1, tiled=True
            )
        part, (previous[-1],) = after(part, previous[-1])
        returned.append(exchange(part))
        previous = returned

    last = chunks - 1
    total = through_first(range(last - 1), total, f32)
    sums = []
    for q in range(last - 1):
        early = grad_of(q)
        if sums:
            early, (sums[-1],) = after(early, sums[-1])
        sums.append(scatter_rows(early))
    total = through_first([last - 1], total, f32)
    middle = grad_of(last - 1)
    returned[last], (total, middle, second_sum, *sums) = after(
        returned[last], total, middle, second_sum, *sums
    )
    grad_one = grad_of(last)
    sums.append(scatter_rows(jnp.concatenate([middle, grad_one], axis=2)))
    first_sum = jnp.concatenate(sums, axis=2).reshape(first_factor.shape)
    input_grad = through_first([last], total, bf16).reshape(seqs, rows, channels)
    return (outputs, input_grad, first_sum, second_sum)


def solution(mesh):
    in_specs = (
        P(("groups", "dp"), "seq", None),
        P(("groups", "dp"), "seq", None),
        P("seq", "dp", None),
        P("seq", "dp", None),
    )
    out_specs = (
        P(("groups", "dp"), "seq", None),
        P(("groups", "dp"), "seq", None),
        P(("groups", "seq"), "dp", None),
        P(("groups", "seq"), "dp", None),
    )
    return jax.shard_map(shards, mesh=mesh, in_specs=in_specs, out_specs=out_specs, check_vma=False)
```
